128 devices in a mesh: prow: 8 (over x_lo, z), pcol: 16 (over y, x_hi, core).
Axes of the slice: x: 4 (x_hi: 2, x_lo: 2; x = x_hi * 2 + x_lo), y: 4, z: 4, core: 2. Of those that a mesh axis runs over, the one named last changes fastest.
Arguments:
- values: float32 [12, 8, 4, 16, 256, 256], P(None, 'prow', None, 'pcol'), may hold values from -6 to 6
- pattern: int32 [12, 8, 4, 16], P(None, 'prow', None, 'pcol'), may hold values from 0 to 1
Outputs:
- factored: float32 [12, 8, 4, 16, 256, 256], P(None, 'prow', None, 'pcol')
The draws below stay inside these ranges and needn't reach their ends.
All inputs are finite; a program needn't handle non-finite values.
Results may differ from the reference program's by a relative error of at most 0.0003.
Values sent between devices are 32-bit elements; how exact they have to be, the bound alone decides.
A program may use at most 128 MiB of HBM per device.

```python
import math
import jax
import jax.numpy as jnp
from jax import lax

B = 256
LR = 12
LC = 4
SWEEPS = 3
N_PROW = 8
N_PCOL = 16


def draw_values(key, part):
    shape = (LR, N_PROW, LC, N_PCOL, B, B)
    return jnp.clip(jax.random.normal(jax.random.fold_in(key, 7), shape, jnp.float32), -6.0, 6.0)


def touch_ends(drawn, rng, low, top_value):
    place = [jax.random.randint(jax.random.fold_in(rng, axis), (), 0, length) for axis, length in enumerate(drawn.shape)]
    longest = drawn.shape.index(max(drawn.shape))
    next_to = place[:longest] + [(place[longest] + 1) % drawn.shape[longest]] + place[longest + 1:]
    return drawn.at[tuple(place)].set(low).at[tuple(next_to)].set(top_value)


def setup_inputs(seed: int = 0) -> dict:
    arg_keys = jax.random.split(jax.random.key(seed), 3)
    return {
        "values": draw_values(jax.random.fold_in(arg_keys[2], 71), 0),
        "pattern": touch_ends(jax.random.randint(arg_keys[1], (LR, N_PROW, LC, N_PCOL), 0, 2), jax.random.fold_in(arg_keys[1], 1), 0, 1).astype(jnp.int32),
    }


shift_coef = 5.0

def newton(block, shift):
    width = block.shape[0]
    eye = jnp.eye(width, dtype=block.dtype)
    approx = eye / shift
    for step in range(SWEEPS):
        inner = jnp.dot(block, approx, precision=lax.Precision.HIGHEST)
        approx = jnp.dot(approx, 2.0 * eye - inner, precision=lax.Precision.HIGHEST)
    return approx

def reference(values, pattern):
    nrow = LR * N_PROW
    ncol = LC * N_PCOL
    width = values.shape[4]
    shift = shift_coef * math.sqrt(width)
    grid = values.reshape(nrow, ncol, width, width) * pattern.reshape(nrow, ncol)[:, :, None, None].astype(values.dtype)
    eye = jnp.eye(width, dtype=values.dtype)
    rows_g = jnp.arange(nrow, dtype=jnp.int32)
    cols_g = jnp.arange(ncol, dtype=jnp.int32)
    diag = rows_g[:, None] == cols_g[None, :]
    grid = grid + jnp.where(diag, shift, 0.0).astype(values.dtype)[:, :, None, None] * eye
    for k in range(2):
        inverse = newton(grid[k, k], shift)
        mult = jnp.einsum('rab,be->rae', grid[:, k], inverse, precision=lax.Precision.HIGHEST)
        upper = grid[k]

        def one_row(item):
            row, lrow, index = item
            product = jnp.einsum('ab,cbe->cae', lrow, upper, precision=lax.Precision.HIGHEST)
            trail = (index > k) & (cols_g > k)
            store = (index > k) & (cols_g == k)
            out = jnp.where(trail[:, None, None], row - product, row)
            return jnp.where(store[:, None, None], lrow[None], out)
        grid = lax.map(one_row, (grid, mult, rows_g))
    return grid.reshape(LR, N_PROW, LC, N_PCOL, width, width)
```

```python
import functools
import math

import jax
import jax.numpy as jnp
from jax import lax
from jax.experimental import pallas as pl
from jax.experimental.pallas import tpu as pltpu
from jax.sharding import PartitionSpec as P

SWEEPS = 3
SHIFT_COEF = 5.0
MESH = pl.DeviceIdType.MESH

TREES = (
    ((0, 0, 1, 0), (1, 0, 2, 0), (1, 0, 1, 1), (2, 0, 3, 0), (1, 1, 2, 1), (1, 1, 0, 1), (2, 1, 3, 1)),
    ((0, 0, 3, 0), (3, 0, 2, 0), (3, 0, 3, 1), (2, 0, 1, 0), (3, 1, 2, 1), (3, 1, 0, 1), (2, 1, 1, 1)),
    ((0, 0, 1, 0), (1, 0, 2, 0), (2, 0, 3, 0), (2, 0, 2, 1), (2, 1, 3, 1), (2, 1, 1, 1), (3, 1, 0, 1)),
    ((0, 0, 3, 0), (0, 0, 0, 1), (3, 0, 2, 0), (0, 1, 1, 1), (0, 1, 3, 1), (2, 0, 1, 0), (1, 1, 2, 1)),
)
NT = len(TREES)


def tree_depths(edges):
    depth = {(0, 0): 0}
    for a, b, c, d in edges:
        depth[c, d] = depth[a, b] + 1
    return depth


DEPTHS = tuple(tree_depths(edges) for edges in TREES)
MAX_DEPTH = max(max(d.values()) for d in DEPTHS)


def lookup(node, table):
    out = jnp.int32(0)
    for (a, b), value in table.items():
        if value:
            out = jnp.where(node == a * 2 + b, jnp.int32(value), out)
    return out


def split(x):
    high = x.astype(jnp.bfloat16)
    return high, (x - high.astype(jnp.float32)).astype(jnp.bfloat16)


def dot(a, b):
    return jnp.dot(a, b, preferred_element_type=jnp.float32)


def mm(a, b):
    ah, al = split(a)
    bh, bl = split(b)
    return dot(ah, bh) + (dot(ah, bl) + dot(al, bh))


def eye_of(width):
    rows = lax.broadcasted_iota(jnp.int32, (width, width), 0)
    cols = lax.broadcasted_iota(jnp.int32, (width, width), 1)
    return jnp.where(rows == cols, 1.0, 0.0).astype(jnp.float32)


def comm_kernel(
    dims, pat, values, cols_out, vh_out, vl_out, fix_out,
    colbuf, rowbuf, piv, vtmp, xs,
    load_sem, col_send, col_recv, row_send, row_recv, piv_send, piv_recv,
    sib_send, sib_recv, sibp_send, sibp_recv, out_sem,
):
    nr, nc, width, shift = dims
    qr = width // NT
    p = lax.axis_index("prow")
    q = lax.axis_index("pcol")
    xlo, z = p // 4, p % 4
    y, xhi, core = q // 4, (q // 2) % 2, q % 2
    other = 1 - core

    def dev(xlo_, z_, y_, xhi_, core_):
        return (xlo_ * 4 + z_, y_ * 4 + xhi_ * 2 + core_)

    sibling = dev(xlo, z, y, xhi, other)
    barrier = pltpu.get_barrier_semaphore()
    partners = (
        sibling,
        dev(xlo, z, (y + 1) % 4, xhi, core),
        dev(xlo, z, (y + 3) % 4, xhi, core),
        dev(xlo, z, y, 1 - xhi, core),
        dev(xlo, (z + 1) % 4, y, xhi, core),
        dev(xlo, (z + 3) % 4, y, xhi, core),
        dev(1 - xlo, z, y, xhi, core),
    )
    for partner in partners:
        pl.semaphore_signal(barrier, inc=1, device_id=partner, device_id_type=MESH)

    cnode = y * 2 + xhi
    cdepth = [lookup(cnode, d) for d in DEPTHS]
    rnode = [((z + 4 - k) % 4) * 2 + xlo for k in range(2)]
    rdepth = [[lookup(rnode[k], d) for d in DEPTHS] for k in range(2)]
    cmax = cdepth[0]
    for d in cdepth[1:]:
        cmax = jnp.maximum(cmax, d)

    def children(tree, node, place):
        kids = {}
        for a, b, c, d in TREES[tree]:
            kids.setdefault((a, b), []).append((c, d))
        out = []
        for slot in range(max(len(v) for v in kids.values())):
            has = {n: 1 for n, v in kids.items() if len(v) > slot}
            to_a = lookup(node, {n: v[slot][0] for n, v in kids.items() if len(v) > slot})
            to_b = lookup(node, {n: v[slot][1] for n, v in kids.items() if len(v) > slot})
            out.append((lookup(node, has) == 1, place(to_a, to_b)))
        return out

    ckids = [children(t, cnode, lambda a, b: dev(xlo, z, a, b, core)) for t in range(NT)]
    rkids = [
        [children(t, rnode[k], lambda a, b, k=k: dev(b, (a + k) % 4, y, xhi, core)) for t in range(NT)]
        for k in range(2)
    ]

    def remote(src, dst, send, recv, device):
        return pltpu.make_async_remote_copy(
            src_ref=src, dst_ref=dst, send_sem=send, recv_sem=recv,
            device_id=device, device_id_type=MESH,
        )

    def send_col(t, u):
        ref = colbuf.at[core, u, pl.ds(t * qr, qr)]
        for slot, (has, device) in enumerate(ckids[t]):
            pl.when(has)(remote(ref, ref, col_send.at[t, slot], col_recv.at[t, u], device).start)

    def send_row(k, t, v):
        ref = rowbuf.at[k, v, pl.ds(t * qr, qr)]
        for slot, (has, device) in enumerate(rkids[k][t]):
            pl.when(has)(remote(ref, ref, row_send.at[k, t, slot], row_recv.at[k, t, v], device).start)

    def send_piv(k, t):
        ref = piv.at[k, core, pl.ds(t * qr, qr)]
        for slot, (has, device) in enumerate(rkids[k][t]):
            pl.when(has)(remote(ref, ref, piv_send.at[k, t, slot], piv_recv.at[k, t], device).start)
        remote(ref, ref, sibp_send.at[k], sibp_recv.at[k, t], sibling).start()

    def sib_copy(u):
        ref = colbuf.at[core, u]
        return remote(ref, ref, sib_send, sib_recv.at[u], sibling)

    def arrive(ref, sem):
        pltpu.make_async_copy(ref, ref, sem).wait()

    eye = eye_of(width)
    col_root = cnode == 0
    row_root = [p == k for k in range(2)]

    @pl.when(col_root)
    def _():
        for u in range(nr):
            pltpu.make_async_copy(values.at[u, 0], colbuf.at[core, u], load_sem.at[u]).start()

    for k in range(2):
        @pl.when(row_root[k])
        def _():
            for v in range(nc):
                pltpu.make_async_copy(values.at[0, v], rowbuf.at[k, v], load_sem.at[nr + v]).start()

    pl.semaphore_wait(barrier, len(partners))

    for k in range(2):
        @pl.when(row_root[k])
        def _():
            for v in range(nc):
                pltpu.make_async_copy(values.at[0, v], rowbuf.at[k, v], load_sem.at[nr + v]).wait()
                block = rowbuf[k, v] * pat[v].astype(jnp.float32)
                if v == 0:
                    block = block + jnp.where(q == k, shift, 0.0).astype(jnp.float32) * eye
                rowbuf[k, v] = block

    def own_piv(k, t):
        piv[k, core, pl.ds(t * qr, qr)] = colbuf[core, 0, pl.ds(t * qr, qr)]
        send_piv(k, t)

    @pl.when(col_root)
    def _():
        def one(u, carry):
            pltpu.make_async_copy(values.at[u, 0], colbuf.at[core, u], load_sem.at[u]).wait()
            on_diag = (u == 0) & (p == core)
            block = colbuf[core, u] * pat[u * nc].astype(jnp.float32)
            colbuf[core, u] = block + jnp.where(on_diag, shift, 0.0).astype(jnp.float32) * eye
            for t in range(NT):
                send_col(t, u)
            sib_copy(u).start()
            return carry

        one(0, 0)
        for k in range(2):
            @pl.when(row_root[k])
            def _():
                for t in range(NT):
                    own_piv(k, t)
        lax.fori_loop(1, nr, one, 0)

    for k in range(2):
        @pl.when(row_root[k])
        def _():
            for v in range(nc):
                for t in range(NT):
                    send_row(k, t, v)

    def relay(s):
        for t in range(NT):
            u = s - cdepth[t]

            @pl.when((cdepth[t] > 0) & (u >= 0) & (u < nr))
            def _():
                arrive(colbuf.at[core, u, pl.ds(t * qr, qr)], col_recv.at[t, u])
                send_col(t, u)

                for k in range(2):
                    @pl.when(row_root[k] & (u == 0))
                    def _():
                        own_piv(k, t)

        for k in range(2):
            for t in range(NT):
                @pl.when((rdepth[k][t] > 0) & (s == cdepth[t] + rdepth[k][t]))
                def _():
                    arrive(piv.at[k, core, pl.ds(t * qr, qr)], piv_recv.at[k, t])
                    send_piv(k, t)

        for k in range(2):
            for t in range(NT):
                w = s - rdepth[k][t]

                @pl.when((rdepth[k][t] > 0) & (w >= 0) & (w < 2 * nc) & (w % 2 == 0))
                def _():
                    v = w // 2
                    arrive(rowbuf.at[k, v, pl.ds(t * qr, qr)], row_recv.at[k, t, v])
                    send_row(k, t, v)

        done = s - cmax

        @pl.when((cmax > 0) & (done >= 0) & (done < nr))
        def _():
            sib_copy(done).start()

    def newton_steps(block_ref, out):
        def first():
            block = block_ref[...]
            xs[out] = (2.0 * eye - block * (1.0 / shift)) * (1.0 / shift)

        def inner():
            xs[4] = 2.0 * eye - mm(block_ref[...], xs[out])

        def outer():
            xs[out] = mm(xs[out], xs[4])

        steps = [first]
        for _ in range(SWEEPS - 1):
            steps += [inner, outer]
        return steps

    def wait_piv():
        for k in range(2):
            for t in range(NT):
                ref = piv.at[k, other, pl.ds(t * qr, qr)]
                arrive(ref, sibp_recv.at[k, t])

    def middle():
        xs[2] = mm(piv[1, 0], xs[0])

    def schur():
        xs[3] = piv[1, 1] - mm(xs[2], piv[0, 1])

    def u_one():
        for c in range(nc):
            vtmp[1, c] = rowbuf[1, c] - mm(xs[2], rowbuf[0, c])

        @pl.when(p == 1)
        def _():
            fix_out[...] = vtmp[1]

            @pl.when(q == 0)
            def _():
                fix_out[0] = xs[2]

        @pl.when(q < 2)
        def _():
            vtmp[1, 0] = jnp.where(q == 1, -1.0, 0.0).astype(jnp.float32) * eye

    def put_v(k, c, value):
        high, low = split(value)
        vh_out[c, pl.ds(k * width, width)] = high
        vl_out[c, pl.ds(k * width, width)] = low

    def v_one():
        for c in range(nc):
            value = mm(xs[1], vtmp[1, c])
            vtmp[1, c] = value
            put_v(1, c, value)

    def v_mid():
        for c in range(nc):
            upper = rowbuf[0, c]
            if c == 0:
                upper = jnp.where(q < 2, jnp.where(q == 0, -1.0, 0.0).astype(jnp.float32) * eye, upper)
            vtmp[0, c] = upper - mm(piv[0, 1], vtmp[1, c])

    def v_zero():
        for c in range(nc):
            put_v(0, c, mm(xs[0], vtmp[0, c]))

    work = [wait_piv]
    work += newton_steps(piv.at[0, 0], 0)
    work += [middle, schur]
    work += newton_steps(xs.at[3], 1)
    tail = [u_one, v_one, v_mid, v_zero]
    first_step = 2 * MAX_DEPTH + 1
    last = max(nr, 2 * nc) + MAX_DEPTH
    slots = max(last - first_step, 1)
    per = -(-len(work) // slots)

    def step(s, carry):
        relay(s)
        for i in range(slots):
            part = work[i * per:(i + 1) * per]
            if part:
                @pl.when(s == first_step + i)
                def _():
                    for item in part:
                        item()
        return carry

    lax.fori_loop(0, last, step, 0)

    def out_copy(k, u):
        return pltpu.make_async_copy(colbuf.at[k, u], cols_out.at[k, u], out_sem)

    for u in range(nr):
        arrive(colbuf.at[other, u], sib_recv.at[u])
    whole = pltpu.make_async_copy(colbuf, cols_out, out_sem)
    whole.start()
    for item in tail:
        item()

    for t in range(NT):
        for slot, (has, _) in enumerate(ckids[t]):
            ref = colbuf.at[0, pl.ds(0, nr), pl.ds(0, qr)]
            pl.when(has)(functools.partial(arrive, ref, col_send.at[t, slot]))
        for k in range(2):
            for slot, (has, _) in enumerate(rkids[k][t]):
                ref = rowbuf.at[0, pl.ds(0, nc), pl.ds(0, qr)]
                pl.when(has)(functools.partial(arrive, ref, row_send.at[k, t, slot]))
                ref = piv.at[0, 0, pl.ds(0, qr)]
                pl.when(has)(functools.partial(arrive, ref, piv_send.at[k, t, slot]))
    arrive(colbuf.at[core], sib_send)
    for k in range(2):
        arrive(piv.at[0, 0], sibp_send.at[k])
    whole.wait()


def update_kernel(dims, pat, values, cols, vh, vl, fix, out):
    nr, nc, width, shift = dims
    r = pl.program_id(0)
    p = lax.axis_index("prow")
    q = lax.axis_index("pcol")
    row = r * 8 + p
    eye = eye_of(width)

    def base(c):
        on_diag = row == c * 16 + q
        block = values[0, c] * pat[r * nc + c].astype(jnp.float32)
        return block + jnp.where(on_diag, shift, 0.0).astype(jnp.float32) * eye

    @pl.when(row == 0)
    def _():
        for c in range(nc):
            out[0, c] = base(c)

    @pl.when(row == 1)
    def _():
        out[0] = fix[...]

    @pl.when(row > 1)
    def _():
        c0h, c0l = split(cols[0, 0])
        c1h, c1l = split(cols[1, 0])
        high = jnp.concatenate([c0h, c1h], axis=1)
        low = jnp.concatenate([c0l, c1l], axis=1)
        for c in range(nc):
            prod = dot(high, vh[c]) + (dot(high, vl[c]) + dot(low, vh[c]))
            keep = base(c)
            if c == 0:
                keep = jnp.where(q < 2, 0.0, 1.0).astype(jnp.float32) * keep
            out[0, c] = keep - prod


def body(values, pattern):
    nr, _, nc, _, width, _ = values.shape
    shift = SHIFT_COEF * math.sqrt(width)
    dims = (nr, nc, width, shift)
    vals = values.reshape(nr, nc, width, width)
    pat = pattern.reshape(nr * nc)
    f32, bf16 = jnp.float32, jnp.bfloat16
    vmem = pl.BlockSpec(memory_space=pltpu.VMEM)
    dma = pltpu.SemaphoreType.DMA
    cols, vh, vl, fix = pl.pallas_call(
        functools.partial(comm_kernel, dims),
        out_shape=(
            jax.ShapeDtypeStruct((2, nr, width, width), f32),
            jax.ShapeDtypeStruct((nc, 2 * width, width), bf16),
            jax.ShapeDtypeStruct((nc, 2 * width, width), bf16),
            jax.ShapeDtypeStruct((nc, width, width), f32),
        ),
        in_specs=[pl.BlockSpec(memory_space=pltpu.SMEM), pl.BlockSpec(memory_space=pl.ANY)],
        out_specs=(pl.BlockSpec(memory_space=pl.ANY), vmem, vmem, vmem),
        scratch_shapes=[
            pltpu.VMEM((2, nr, width, width), f32),
            pltpu.VMEM((2, nc, width, width), f32),
            pltpu.VMEM((2, 2, width, width), f32),
            pltpu.VMEM((2, nc, width, width), f32),
            pltpu.VMEM((5, width, width), f32),
            dma((nr + nc,)),
            dma((NT, 2)),
            dma((NT, nr)),
            dma((2, NT, 2)),
            dma((2, NT, nc)),
            dma((2, NT, 2)),
            dma((2, NT)),
            dma,
            dma((nr,)),
            dma((2,)),
            dma((2, NT)),
            dma,
        ],
        compiler_params=pltpu.CompilerParams(
            collective_id=0, has_side_effects=True, vmem_limit_bytes=40 << 20
        ),
        name="gather_panels",
    )(pat, vals)
    whole = lambda *shape: pl.BlockSpec(shape, lambda r: (0,) * len(shape))
    out = pl.pallas_call(
        functools.partial(update_kernel, dims),
        grid=(nr,),
        out_shape=jax.ShapeDtypeStruct((nr, nc, width, width), f32),
        in_specs=[
            pl.BlockSpec(memory_space=pltpu.SMEM),
            pl.BlockSpec((1, nc, width, width), lambda r: (r, 0, 0, 0)),
            pl.BlockSpec((2, 1, width, width), lambda r: (0, r, 0, 0)),
            whole(nc, 2 * width, width),
            whole(nc, 2 * width, width),
            whole(nc, width, width),
        ],
        out_specs=pl.BlockSpec((1, nc, width, width), lambda r: (r, 0, 0, 0)),
        compiler_params=pltpu.CompilerParams(vmem_limit_bytes=40 << 20),
        cost_estimate=pl.CostEstimate(flops=6 * nr * nc * width**3 * 2, bytes_accessed=35 << 20, transcendentals=0),
        name="update_blocks",
    )(pat, vals, cols, vh, vl, fix)
    return out.reshape(values.shape)


def solution(mesh):
    return jax.shard_map(
        body,
        mesh=mesh,
        in_specs=(P(None, "prow", None, "pcol", None, None), P(None, "prow", None, "pcol")),
        out_specs=P(None, "prow", None, "pcol", None, None),
        check_vma=False,
    )
```

```python
import functools
import math

import jax
import jax.numpy as jnp
from jax import lax
from jax.experimental import pallas as pl
from jax.experimental.pallas import tpu as pltpu
from jax.sharding import PartitionSpec as P

SWEEPS = 3
SHIFT_COEF = 5.0
MESH = pl.DeviceIdType.MESH

COL_TREES = (
    ((0, 0, 1, 0), (1, 0, 2, 0), (1, 0, 1, 1), (2, 0, 3, 0), (2, 0, 2, 1), (1, 1, 0, 1), (2, 1, 3, 1)),
    ((0, 0, 3, 0), (3, 0, 2, 0), (3, 0, 3, 1), (2, 0, 1, 0), (3, 1, 2, 1), (3, 1, 0, 1), (2, 1, 1, 1)),
    ((0, 0, 0, 1), (0, 1, 1, 1), (0, 1, 3, 1), (1, 1, 2, 1), (1, 1, 1, 0), (3, 1, 3, 0), (2, 1, 2, 0)),
)
NC_TREES = len(COL_TREES)
TREES = (
    ((0, 0, 1, 0), (1, 0, 2, 0), (1, 0, 1, 1), (2, 0, 3, 0), (1, 1, 2, 1), (1, 1, 0, 1), (2, 1, 3, 1)),
    ((0, 0, 3, 0), (3, 0, 2, 0), (3, 0, 3, 1), (2, 0, 1, 0), (3, 1, 2, 1), (3, 1, 0, 1), (2, 1, 1, 1)),
    ((0, 0, 1, 0), (1, 0, 2, 0), (2, 0, 3, 0), (2, 0, 2, 1), (2, 1, 3, 1), (2, 1, 1, 1), (3, 1, 0, 1)),
    ((0, 0, 3, 0), (0, 0, 0, 1), (3, 0, 2, 0), (0, 1, 1, 1), (0, 1, 3, 1), (2, 0, 1, 0), (1, 1, 2, 1)),
)
NT = len(TREES)
HOP = 3
ROW_STEP = 4
ROW_BASE = 4
PIV_BASE = 13
PACE = 4
SLOTS = 3


def tree_depths(edges):
    depth = {(0, 0): 0}
    for a, b, c, d in edges:
        depth[c, d] = depth[a, b] + 1
    return depth


COL_DEPTHS = tuple(tree_depths(edges) for edges in COL_TREES)
DEPTHS = tuple(tree_depths(edges) for edges in TREES)
COL_DEPTH = max(max(d.values()) for d in COL_DEPTHS)
ROW_DEPTH = max(max(d.values()) for d in DEPTHS)


def lookup(node, table):
    out = jnp.int32(0)
    for (a, b), value in table.items():
        if value:
            out = jnp.where(node == a * 2 + b, jnp.int32(value), out)
    return out


def split(x):
    high = x.astype(jnp.bfloat16)
    return high, (x - high.astype(jnp.float32)).astype(jnp.bfloat16)


def dot(a, b):
    return jnp.dot(a, b, preferred_element_type=jnp.float32)


def mm(a, b):
    ah, al = split(a)
    bh, bl = split(b)
    return dot(ah, bh) + (dot(ah, bl) + dot(al, bh))


def eye_of(width):
    rows = lax.broadcasted_iota(jnp.int32, (width, width), 0)
    cols = lax.broadcasted_iota(jnp.int32, (width, width), 1)
    return jnp.where(rows == cols, 1.0, 0.0).astype(jnp.float32)


def comm_kernel(
    dims, pat, values, colbuf, own, vh_out, vl_out, fix_out, flags,
    rowbuf, piv, vtmp, xs,
    own_sem, load_sem, root_sem, col_send, col_recv, row_send, row_recv, piv_send, piv_recv,
    sib_send, sib_recv, sibp_send, sibp_recv,
):
    nr, nc, width, shift = dims
    qr = width // NT
    p = lax.axis_index("prow")
    q = lax.axis_index("pcol")
    xlo, z = p // 4, p % 4
    y, xhi, core = q // 4, (q // 2) % 2, q % 2
    other = 1 - core

    def dev(xlo_, z_, y_, xhi_, core_):
        return (xlo_ * 4 + z_, y_ * 4 + xhi_ * 2 + core_)

    sibling = dev(xlo, z, y, xhi, other)
    barrier = pltpu.get_barrier_semaphore()
    partners = (
        sibling,
        dev(xlo, z, (y + 1) % 4, xhi, core),
        dev(xlo, z, (y + 3) % 4, xhi, core),
        dev(xlo, z, y, 1 - xhi, core),
        dev(xlo, (z + 1) % 4, y, xhi, core),
        dev(xlo, (z + 3) % 4, y, xhi, core),
        dev(1 - xlo, z, y, xhi, core),
    )
    for partner in partners:
        pl.semaphore_signal(barrier, inc=1, device_id=partner, device_id_type=MESH)

    cnode = y * 2 + xhi
    cdepth = [lookup(cnode, d) for d in COL_DEPTHS]
    rnode = [((z + 4 - k) % 4) * 2 + xlo for k in range(2)]
    rdepth = [[lookup(rnode[k], d) for d in DEPTHS] for k in range(2)]
    chunks = nr * NT // NC_TREES

    def children(edges, node, place):
        kids = {}
        for a, b, c, d in edges:
            kids.setdefault((a, b), []).append((c, d))
        out = []
        for slot in range(max(len(v) for v in kids.values())):
            has = {n: 1 for n, v in kids.items() if len(v) > slot}
            to_a = lookup(node, {n: v[slot][0] for n, v in kids.items() if len(v) > slot})
            to_b = lookup(node, {n: v[slot][1] for n, v in kids.items() if len(v) > slot})
            out.append((lookup(node, has) == 1, place(to_a, to_b)))
        return out

    ckids = [children(e, cnode, lambda a, b: dev(xlo, z, a, b, core)) for e in COL_TREES]
    rkids = [
        [children(e, rnode[k], lambda a, b, k=k: dev(b, (a + k) % 4, y, xhi, core)) for e in TREES]
        for k in range(2)
    ]

    def remote(src, dst, send, recv, device):
        return pltpu.make_async_remote_copy(
            src_ref=src, dst_ref=dst, send_sem=send, recv_sem=recv,
            device_id=device, device_id_type=MESH,
        )

    def col_chunk(t, n):
        return colbuf.at[core, NC_TREES * (n // NT) + t, pl.ds((n % NT) * qr, qr)]

    def send_col(t, n):
        ref = col_chunk(t, n)
        for slot, (has, device) in enumerate(ckids[t]):
            pl.when(has)(remote(ref, ref, col_send.at[t, slot], col_recv.at[t, n], device).start)

    def send_row(k, t, v):
        ref = rowbuf.at[k, v, pl.ds(t * qr, qr)]
        for slot, (has, device) in enumerate(rkids[k][t]):
            pl.when(has)(remote(ref, ref, row_send.at[k, t, slot], row_recv.at[k, t, v], device).start)

    def send_piv(k, t):
        ref = piv.at[k, core, pl.ds(t * qr, qr)]
        for slot, (has, device) in enumerate(rkids[k][t]):
            pl.when(has)(remote(ref, ref, piv_send.at[k, t, slot], piv_recv.at[k, t], device).start)
        remote(ref, ref, sibp_send.at[k], sibp_recv.at[k, t], sibling).start()

    def sib_copy(u):
        ref = colbuf.at[core, u]
        return remote(ref, ref, sib_send, sib_recv.at[u], sibling)

    def arrive(ref, sem):
        pltpu.make_async_copy(ref, ref, sem).wait()

    eye = eye_of(width)
    col_root = cnode == 0
    row_root = [p == k for k in range(2)]

    @pl.when(col_root)
    def _():
        for u in range(nr):
            pltpu.make_async_copy(values.at[u, 0], colbuf.at[core, u], load_sem.at[u]).start()

    for k in range(2):
        @pl.when(row_root[k])
        def _():
            for v in range(nc):
                pltpu.make_async_copy(values.at[0, v], rowbuf.at[k, v], load_sem.at[nr + v]).start()

    for u in range(nr):
        pltpu.make_async_copy(values.at[u], own.at[u], own_sem.at[u]).start()

    pl.semaphore_wait(barrier, len(partners))

    for k in range(2):
        @pl.when(row_root[k])
        def _():
            for v in range(nc):
                pltpu.make_async_copy(values.at[0, v], rowbuf.at[k, v], load_sem.at[nr + v]).wait()
                block = rowbuf[k, v] * pat[v].astype(jnp.float32)
                if v == 0:
                    block = block + jnp.where(q == k, shift, 0.0).astype(jnp.float32) * eye
                rowbuf[k, v] = block

    def own_piv(k, t):
        piv[k, core, pl.ds(t * qr, qr)] = colbuf[core, 0, pl.ds(t * qr, qr)]
        send_piv(k, t)

    def one(u):
        pltpu.make_async_copy(values.at[u, 0], colbuf.at[core, u], load_sem.at[u]).wait()
        on_diag = (u == 0) & (p == core)
        block = colbuf[core, u] * pat[u * nc].astype(jnp.float32)
        colbuf[core, u] = block + jnp.where(on_diag, shift, 0.0).astype(jnp.float32) * eye

    for k in range(2):
        @pl.when(row_root[k])
        def _():
            for v in range(nc // 2):
                for t in range(NT):
                    send_row(k, t, v)

    def root_send(t, n):
        ref = col_chunk(t, n)
        return remote(ref, ref, root_sem.at[t, n], col_recv.at[t, n], ckids[t][0][1])

    def relay(s):
        for k in range(2):
            @pl.when(row_root[k] & (s == ROW_STEP))
            def _():
                for v in range(nc // 2, nc):
                    for t in range(NT):
                        send_row(k, t, v)

        for t in range(NC_TREES):
            n = s - HOP * cdepth[t]

            @pl.when((n >= 0) & (n < chunks))
            def _():
                @pl.when(cdepth[t] > 0)
                def _():
                    arrive(col_chunk(t, n), col_recv.at[t, n])
                    send_col(t, n)

                @pl.when(cdepth[t] == 0)
                def _():
                    @pl.when(n % NT == 0)
                    def _():
                        one(NC_TREES * (n // NT) + t)

                    @pl.when(n >= PACE)
                    def _():
                        root_send(t, n - PACE).wait_send()

                    root_send(t, n).start()

                @pl.when(n % NT == NT - 1)
                def _():
                    sib_copy(NC_TREES * (n // NT) + t).start()

                if t == 0:
                    for i in range(NT):
                        for k in range(2):
                            @pl.when(row_root[k] & (n == i))
                            def _():
                                own_piv(k, i)

        for k in range(2):
            for t in range(NT):
                @pl.when((rdepth[k][t] > 0) & (s == PIV_BASE + HOP * rdepth[k][t]))
                def _():
                    arrive(piv.at[k, core, pl.ds(t * qr, qr)], piv_recv.at[k, t])
                    send_piv(k, t)

        for k in range(2):
            for t in range(NT):
                w = s - ROW_BASE - HOP * rdepth[k][t]

                @pl.when((rdepth[k][t] > 0) & (w >= 0) & (w < ROW_STEP * nc) & (w % ROW_STEP == 0))
                def _():
                    v = w // ROW_STEP
                    arrive(rowbuf.at[k, v, pl.ds(t * qr, qr)], row_recv.at[k, t, v])
                    send_row(k, t, v)

    def newton_steps(block_ref, out):
        def first():
            block = block_ref[...]
            xs[out] = (2.0 * eye - block * (1.0 / shift)) * (1.0 / shift)

        def inner():
            xs[4] = 2.0 * eye - mm(block_ref[...], xs[out])

        def outer():
            xs[out] = mm(xs[out], xs[4])

        steps = [first]
        for _ in range(SWEEPS - 1):
            steps += [inner, outer]
        return steps

    def wait_piv():
        for k in range(2):
            for t in range(NT):
                ref = piv.at[k, other, pl.ds(t * qr, qr)]
                arrive(ref, sibp_recv.at[k, t])

    def middle():
        xs[2] = mm(piv[1, 0], xs[0])

    def schur():
        xs[3] = piv[1, 1] - mm(xs[2], piv[0, 1])

    def u_one():
        for c in range(nc):
            vtmp[1, c] = rowbuf[1, c] - mm(xs[2], rowbuf[0, c])

        @pl.when(p == 1)
        def _():
            fix_out[...] = vtmp[1]

            @pl.when(q == 0)
            def _():
                fix_out[0] = xs[2]

        @pl.when(q < 2)
        def _():
            vtmp[1, 0] = jnp.where(q == 1, -1.0, 0.0).astype(jnp.float32) * eye

    def put_v(k, c, value):
        high, low = split(value)
        vh_out[c, pl.ds(k * width, width)] = high
        vl_out[c, pl.ds(k * width, width)] = low

    def v_one():
        for c in range(nc):
            value = mm(xs[1], vtmp[1, c])
            vtmp[1, c] = value
            put_v(1, c, value)

    def v_mid():
        for c in range(nc):
            upper = rowbuf[0, c]
            if c == 0:
                upper = jnp.where(q < 2, jnp.where(q == 0, -1.0, 0.0).astype(jnp.float32) * eye, upper)
            vtmp[0, c] = upper - mm(piv[0, 1], vtmp[1, c])

    def v_zero():
        for c in range(nc):
            put_v(0, c, mm(xs[0], vtmp[0, c]))

    work = [wait_piv]
    work += newton_steps(piv.at[0, 0], 0)
    work += [middle, schur]
    work += newton_steps(xs.at[3], 1)
    tail = [u_one, v_one, v_mid, v_zero]
    first_step = PIV_BASE + HOP * ROW_DEPTH + 1
    last = max(chunks + HOP * COL_DEPTH, ROW_BASE + ROW_STEP * (nc - 1) + HOP * ROW_DEPTH + 1)
    slots = max(last - first_step, 1)
    per = -(-len(work) // slots)

    def step(s, carry):
        relay(s)
        for i in range(slots):
            part = work[i * per:(i + 1) * per]
            if part:
                @pl.when(s == first_step + i)
                def _():
                    for item in part:
                        item()
        return carry

    lax.fori_loop(0, last, step, 0)

    for u in range(nr):
        arrive(colbuf.at[other, u], sib_recv.at[u])
    for item in tail:
        item()

    def mark(u, carry):
        for k in range(2):
            flags[k * nr + u] = jnp.max(jnp.abs(colbuf[k, u]))
        return carry

    lax.fori_loop(0, nr, mark, 0)
    for u in range(nr):
        pltpu.make_async_copy(values.at[u], own.at[u], own_sem.at[u]).wait()

    for t in range(NC_TREES):
        for slot, (has, _) in enumerate(ckids[t]):
            ref = colbuf.at[0, pl.ds(0, nr // NC_TREES)]
            pl.when(has & (cnode > 0))(functools.partial(arrive, ref, col_send.at[t, slot]))

        @pl.when(col_root)
        def _():
            for n in range(chunks - PACE, chunks):
                root_send(t, n).wait_send()
    for t in range(NT):
        for k in range(2):
            for slot, (has, _) in enumerate(rkids[k][t]):
                ref = rowbuf.at[0, pl.ds(0, nc), pl.ds(0, qr)]
                pl.when(has)(functools.partial(arrive, ref, row_send.at[k, t, slot]))
                ref = piv.at[0, 0, pl.ds(0, qr)]
                pl.when(has)(functools.partial(arrive, ref, piv_send.at[k, t, slot]))
    arrive(colbuf.at[core], sib_send)
    for k in range(2):
        arrive(piv.at[0, 0], sibp_send.at[k])


def update_kernel(dims, pat, flags, values, cols, vh, vl, fix, out, stage, sem):
    nr, nc, width, shift = dims
    p = lax.axis_index("prow")
    q = lax.axis_index("pcol")

    def out_copy(r):
        return pltpu.make_async_copy(stage.at[r % SLOTS], out.at[r], sem.at[r % SLOTS])

    def step(r, carry):
        slot = r % SLOTS
        row = r * 8 + p

        @pl.when(r >= SLOTS)
        def _():
            out_copy(r - SLOTS).wait()

        for c in range(nc):
            keep = pat[r * nc + c].astype(jnp.float32)
            if c == 0:
                keep = jnp.where((q < 2) & (row > 1), 0.0, keep)
            stage[slot, c] = values[r, c] * keep

            @pl.when(row == c * 16 + q)
            def _():
                stage[slot, c] += shift * eye_of(width)

        def subtract(part):
            high, low = split(part())
            rows = {2: slice(0, 2 * width), 0: slice(0, width), 1: slice(width, 2 * width)}[part.which]
            for c in range(nc):
                prod = dot(high, vh[c, rows]) + (dot(high, vl[c, rows]) + dot(low, vh[c, rows]))
                stage[slot, c] -= prod

        first = flags[r] > 0
        second = flags[nr + r] > 0
        trail = row > 1

        def both():
            return jnp.concatenate([cols[0, r], cols[1, r]], axis=1)

        def only_first():
            return cols[0, r]

        def only_second():
            return cols[1, r]

        both.which, only_first.which, only_second.which = 2, 0, 1
        pl.when(trail & first & second)(lambda: subtract(both))
        pl.when(trail & first & jnp.logical_not(second))(lambda: subtract(only_first))
        pl.when(trail & jnp.logical_not(first) & second)(lambda: subtract(only_second))

        @pl.when(row == 1)
        def _():
            stage[slot] = fix[...]

        out_copy(r).start()
        return carry

    lax.fori_loop(0, nr, step, 0)
    for r in range(nr - SLOTS, nr):
        out_copy(r).wait()


def body(values, pattern):
    nr, _, nc, _, width, _ = values.shape
    shift = SHIFT_COEF * math.sqrt(width)
    dims = (nr, nc, width, shift)
    vals = values.reshape(nr, nc, width, width)
    pat = pattern.reshape(nr * nc)
    f32, bf16 = jnp.float32, jnp.bfloat16
    vmem = pl.BlockSpec(memory_space=pltpu.VMEM)
    dma = pltpu.SemaphoreType.DMA
    smem = pl.BlockSpec(memory_space=pltpu.SMEM)
    anywhere = pl.BlockSpec(memory_space=pl.ANY)
    *held, flags = pl.pallas_call(
        functools.partial(comm_kernel, dims),
        out_shape=(
            pltpu.VMEM((2, nr, width, width), f32),
            pltpu.VMEM((nr, nc, width, width), f32),
            pltpu.VMEM((nc, 2 * width, width), bf16),
            pltpu.VMEM((nc, 2 * width, width), bf16),
            pltpu.VMEM((nc, width, width), f32),
            jax.ShapeDtypeStruct((2 * nr,), f32),
        ),
        in_specs=[smem, anywhere],
        out_specs=(vmem, vmem, vmem, vmem, vmem, smem),
        scratch_shapes=[
            pltpu.VMEM((2, nc, width, width), f32),
            pltpu.VMEM((2, 2, width, width), f32),
            pltpu.VMEM((2, nc, width, width), f32),
            pltpu.VMEM((5, width, width), f32),
            dma((nr,)),
            dma((nr + nc,)),
            dma((NC_TREES, nr * NT // NC_TREES)),
            dma((NC_TREES, 2)),
            dma((NC_TREES, nr * NT // NC_TREES)),
            dma((2, NT, 2)),
            dma((2, NT, nc)),
            dma((2, NT, 2)),
            dma((2, NT)),
            dma,
            dma((nr,)),
            dma((2,)),
            dma((2, NT)),
        ],
        compiler_params=pltpu.CompilerParams(
            collective_id=0, has_side_effects=True, vmem_limit_bytes=40 << 20
        ),
        name="gather_panels",
    )(pat, vals)
    cols, own, vh, vl, fix = [pltpu.with_memory_space_constraint(x, pltpu.VMEM) for x in held]
    out = pl.pallas_call(
        functools.partial(update_kernel, dims),
        out_shape=jax.ShapeDtypeStruct((nr, nc, width, width), f32),
        in_specs=[smem, smem, vmem, vmem, vmem, vmem, vmem],
        out_specs=anywhere,
        scratch_shapes=[pltpu.VMEM((SLOTS, nc, width, width), f32), dma((SLOTS,))],
        compiler_params=pltpu.CompilerParams(vmem_limit_bytes=40 << 20),
        name="update_blocks",
    )(pat, flags, own, cols, vh, vl, fix)
    return out.reshape(values.shape)


def solution(mesh):
    return jax.shard_map(
        body,
        mesh=mesh,
        in_specs=(P(None, "prow", None, "pcol", None, None), P(None, "prow", None, "pcol")),
        out_specs=P(None, "prow", None, "pcol", None, None),
        check_vma=False,
    )
```

```python
import functools
import math

import jax
import jax.numpy as jnp
from jax import lax
from jax.experimental import pallas as pl
from jax.experimental.pallas import tpu as pltpu
from jax.sharding import PartitionSpec as P

SWEEPS = 3
SHIFT_COEF = 5.0
MESH = pl.DeviceIdType.MESH

COL_TREES = (
    ((0, 0, 1, 0), (1, 0, 2, 0), (1, 0, 1, 1), (2, 0, 3, 0), (2, 0, 2, 1), (1, 1, 0, 1), (2, 1, 3, 1)),
    ((0, 0, 3, 0), (3, 0, 2, 0), (3, 0, 3, 1), (2, 0, 1, 0), (3, 1, 2, 1), (3, 1, 0, 1), (2, 1, 1, 1)),
    ((0, 0, 0, 1), (0, 1, 1, 1), (0, 1, 3, 1), (1, 1, 2, 1), (1, 1, 1, 0), (3, 1, 3, 0), (2, 1, 2, 0)),
)
NC_TREES = len(COL_TREES)
TREES = (
    ((0, 0, 1, 0), (1, 0, 2, 0), (1, 0, 1, 1), (2, 0, 3, 0), (1, 1, 2, 1), (1, 1, 0, 1), (2, 1, 3, 1)),
    ((0, 0, 3, 0), (3, 0, 2, 0), (3, 0, 3, 1), (2, 0, 1, 0), (3, 1, 2, 1), (3, 1, 0, 1), (2, 1, 1, 1)),
    ((0, 0, 1, 0), (1, 0, 2, 0), (2, 0, 3, 0), (2, 0, 2, 1), (2, 1, 3, 1), (2, 1, 1, 1), (3, 1, 0, 1)),
    ((0, 0, 3, 0), (0, 0, 0, 1), (3, 0, 2, 0), (0, 1, 1, 1), (0, 1, 3, 1), (2, 0, 1, 0), (1, 1, 2, 1)),
)
NT = len(TREES)
HOP = 4
ROW_HOP = 2
ROW_STEP = 3
PACE = 4
XS = 4
OWN_AT = 3
SLOTS = 3


def tree_depths(edges):
    depth = {(0, 0): 0}
    for a, b, c, d in edges:
        depth[c, d] = depth[a, b] + 1
    return depth


COL_DEPTHS = tuple(tree_depths(edges) for edges in COL_TREES)
DEPTHS = tuple(tree_depths(edges) for edges in TREES)
COL_DEPTH = max(max(d.values()) for d in COL_DEPTHS)
ROW_DEPTH = max(max(d.values()) for d in DEPTHS)


def lookup(node, table):
    out = jnp.int32(0)
    for (a, b), value in table.items():
        if value:
            out = jnp.where(node == a * 2 + b, jnp.int32(value), out)
    return out


def split(x):
    high = x.astype(jnp.bfloat16)
    return high, (x - high.astype(jnp.float32)).astype(jnp.bfloat16)


def dot(a, b):
    return jnp.dot(a, b, preferred_element_type=jnp.float32)


def mm(a, b):
    ah, al = split(a)
    bh, bl = split(b)
    return dot(ah, bh) + (dot(ah, bl) + dot(al, bh))


def eye_of(width):
    rows = lax.broadcasted_iota(jnp.int32, (width, width), 0)
    cols = lax.broadcasted_iota(jnp.int32, (width, width), 1)
    return jnp.where(rows == cols, 1.0, 0.0).astype(jnp.float32)


def comm_kernel(
    dims, pat, values, colbuf, own, vh_out, vl_out, fix_out, flags,
    rowbuf, vtmp, xs,
    own_sem, load_sem, root_sem, col_send, col_recv, sib_send, sib_recv,
    row_send, row_recv, src_send, src_recv, give_send, give_recv,
    x_send, x_recv, xs_send, xs_recv, xsib_send, xsib_recv,
):
    nr, nc, width, shift = dims
    qr = width // NT
    chunks = nr * NT // NC_TREES
    p = lax.axis_index("prow")
    q = lax.axis_index("pcol")
    xlo, z = p // 4, p % 4
    y, xhi, core = q // 4, (q // 2) % 2, q % 2

    def dev(xlo_, z_, y_, xhi_, core_):
        return (xlo_ * 4 + z_, y_ * 4 + xhi_ * 2 + core_)

    sibling = dev(xlo, z, y, xhi, 1 - core)
    barrier = pltpu.get_barrier_semaphore()
    partners = (
        sibling,
        dev(xlo, z, (y + 1) % 4, xhi, core),
        dev(xlo, z, (y + 3) % 4, xhi, core),
        dev(xlo, z, y, 1 - xhi, core),
        dev(xlo, (z + 1) % 4, y, xhi, core),
        dev(xlo, (z + 3) % 4, y, xhi, core),
        dev(1 - xlo, z, y, xhi, core),
    )
    for partner in partners:
        pl.semaphore_signal(barrier, inc=1, device_id=partner, device_id_type=MESH)

    cnode = y * 2 + xhi
    cdepth = [lookup(cnode, d) for d in COL_DEPTHS]
    rnode = [((z + 4 - k) % 4) * 2 + xlo for k in range(2)]
    rdepth = [[lookup(rnode[k], d) for d in DEPTHS] for k in range(2)]

    def children(edges, node, place):
        kids = {}
        for a, b, c, d in edges:
            kids.setdefault((a, b), []).append((c, d))
        out = []
        for slot in range(max(len(v) for v in kids.values())):
            has = {n: 1 for n, v in kids.items() if len(v) > slot}
            to_a = lookup(node, {n: v[slot][0] for n, v in kids.items() if len(v) > slot})
            to_b = lookup(node, {n: v[slot][1] for n, v in kids.items() if len(v) > slot})
            out.append((lookup(node, has) == 1, place(to_a, to_b)))
        return out

    ckids = [children(e, cnode, lambda a, b: dev(xlo, z, a, b, core)) for e in COL_TREES]
    rkids = [
        [children(e, rnode[k], lambda a, b, k=k: dev(b, (a + k) % 4, y, xhi, core)) for e in TREES]
        for k in range(2)
    ]

    def remote(src, dst, send, recv, device):
        return pltpu.make_async_remote_copy(
            src_ref=src, dst_ref=dst, send_sem=send, recv_sem=recv,
            device_id=device, device_id_type=MESH,
        )

    def arrive(ref, sem):
        pltpu.make_async_copy(ref, ref, sem).wait()

    eye = eye_of(width)
    col_root = cnode == 0
    row_root = [p == k for k in range(2)]
    column_core, row_core = core == 0, core == 1

    def block_of(n, t):
        return NC_TREES * (n // NT) + t

    def col_chunk(j, t, n):
        return colbuf.at[j, block_of(n, t), pl.ds((n % NT) * qr, qr)]

    def send_col(j, t, n):
        ref = col_chunk(j, t, n)
        for slot, (has, device) in enumerate(ckids[t]):
            pl.when(has)(remote(ref, ref, col_send.at[j, t, slot], col_recv.at[j, t, n], device).start)

    def root_send(j, t, n):
        ref = col_chunk(j, t, n)
        return remote(ref, ref, root_sem.at[j, t, n], col_recv.at[j, t, n], ckids[t][0][1])

    def sib_copy(j, u):
        ref = colbuf.at[j, u]
        return remote(ref, ref, sib_send.at[j], sib_recv.at[j, u], sibling)

    def send_row(k, t, v):
        for h in range(2):
            ref = rowbuf.at[k, h, v, pl.ds(t * qr, qr)]
            for slot, (has, device) in enumerate(rkids[k][t]):
                sems = row_send.at[k, h, t, slot], row_recv.at[k, h, t, v]
                pl.when(has)(remote(ref, ref, *sems, device).start)

    def xs_chunk(m):
        return xs.at[m // NT, pl.ds((m % NT) * qr, qr)]

    def send_xs(t, m):
        ref = xs_chunk(m)
        for slot, (has, device) in enumerate(ckids[t]):
            pl.when(has)(remote(ref, ref, xs_send.at[t, slot], xs_recv.at[m], device).start)

    def src_copy(k, v):
        ref = rowbuf.at[k, 0, v]
        return remote(ref, ref, src_send.at[k], src_recv.at[k, v], sibling)

    def give_copy(k, t):
        ref = rowbuf.at[k, 0, pl.ds(0, nc), pl.ds(t * qr, qr)]
        return remote(ref, ref, give_send.at[k], give_recv.at[k, t], sibling)

    def x_copy(i):
        ref = xs.at[i]
        return remote(ref, ref, x_send.at[i], x_recv.at[i], sibling)

    def load_col(u):
        return pltpu.make_async_copy(values.at[u, 0], colbuf.at[core, u], load_sem.at[u])

    def load_row(k, v):
        return pltpu.make_async_copy(values.at[0, v], rowbuf.at[k, core, v], load_sem.at[nr + v])

    def load_own(u):
        return pltpu.make_async_copy(values.at[u], own.at[u], own_sem.at[u])

    def ready_col(u):
        load_col(u).wait()
        on_diag = (u == 0) & (p == core)
        block = colbuf[core, u] * pat[u * nc].astype(jnp.float32)
        colbuf[core, u] = block + jnp.where(on_diag, shift, 0.0).astype(jnp.float32) * eye

    def ready_own(u):
        load_own(u).wait()
        row = u * 8 + p
        for c in range(nc):
            keep = pat[u * nc + c].astype(jnp.float32)
            if c == 0:
                keep = jnp.where((q < 2) & (row > 1), 0.0, keep)
            own[u, c] = own[u, c] * keep

            @pl.when(row == c * 16 + q)
            def _():
                own[u, c] += shift * eye

    @pl.when(col_root)
    def _():
        for u in range(nr):
            load_col(u).start()

    for k in range(2):
        @pl.when(row_root[k])
        def _():
            for v in range(nc):
                load_row(k, v).start()

    for u in range(nr):
        load_own(u).start()

    pl.semaphore_wait(barrier, len(partners))

    @pl.when(col_root & row_core)
    def _():
        def one(u, carry):
            ready_col(u)
            sib_copy(1, u).start()
            return carry

        lax.fori_loop(0, nr, one, 0)

    for k in range(2):
        @pl.when(row_root[k])
        def _():
            for v in range(nc):
                load_row(k, v).wait()
                block = rowbuf[k, core, v] * pat[v].astype(jnp.float32)
                if v == 0:
                    block = block + jnp.where(q == k, shift, 0.0).astype(jnp.float32) * eye
                rowbuf[k, core, v] = block

                @pl.when(column_core)
                def _():
                    src_copy(k, v).start()

    def mark(j, u):
        flags[j * nr + u] = jnp.max(jnp.abs(colbuf[j, u]))

    xs_count = XS * NT
    xs_rounds = -(-xs_count // NC_TREES)

    def col_step(s, carry):
        pl.when((s >= OWN_AT) & (s < OWN_AT + nr))(lambda: ready_own(s - OWN_AT))
        for t in range(NC_TREES):
            n = s - HOP * cdepth[t]
            m = (n - chunks) * NC_TREES + t

            @pl.when((n >= chunks) & (m < xs_count))
            def _():
                @pl.when(cdepth[t] > 0)
                def _():
                    arrive(xs_chunk(m), xs_recv.at[m])

                if t == 0:
                    @pl.when((cdepth[t] == 0) & (n == chunks))
                    def _():
                        for i in range(XS):
                            arrive(xs.at[i], x_recv.at[i])

                send_xs(t, m)

                @pl.when(cdepth[t] > 0)
                def _():
                    ref = xs_chunk(m)
                    remote(ref, ref, xsib_send, xsib_recv.at[m], sibling).start()

            @pl.when((n >= 0) & (n < chunks))
            def _():
                u = block_of(n, t)
                for j in range(2):
                    @pl.when(cdepth[t] > 0)
                    def _():
                        arrive(col_chunk(j, t, n), col_recv.at[j, t, n])
                        send_col(j, t, n)

                        @pl.when(n % NT == NT - 1)
                        def _():
                            sib_copy(j, u).start()
                            mark(j, u)

                    @pl.when(cdepth[t] == 0)
                    def _():
                        @pl.when(n % NT == 0)
                        def _():
                            if j == 0:
                                ready_col(u)
                                sib_copy(0, u).start()
                            else:
                                arrive(colbuf.at[1, u], sib_recv.at[1, u])
                            mark(j, u)

                        @pl.when(n >= PACE)
                        def _():
                            root_send(j, t, n - PACE).wait_send()

                        root_send(j, t, n).start()

        return carry

    def newton_steps(block_ref, out):
        def first():
            block = block_ref[...]
            xs[out] = (2.0 * eye - block * (1.0 / shift)) * (1.0 / shift)

        def inner():
            xs[5] = 2.0 * eye - mm(block_ref[...], xs[out])

        def outer():
            xs[out] = mm(xs[out], xs[5])

        steps = [first]
        for _ in range(SWEEPS - 1):
            steps += [inner, outer]
        return steps

    def middle():
        xs[2] = mm(rowbuf[1, 0, 0], xs[0])

    def schur():
        xs[4] = rowbuf[1, 1, 0] - mm(xs[2], rowbuf[0, 1, 0])

    def corner():
        xs[3] = rowbuf[0, 1, 0]
        x_copy(3).start()

    work = [corner]
    work += newton_steps(rowbuf.at[0, 0, 0], 0)
    work += [x_copy(0).start, middle, x_copy(2).start, schur]
    work += newton_steps(xs.at[4], 1)
    work += [x_copy(1).start]

    work_at = ROW_HOP * ROW_DEPTH
    row_last = ROW_STEP * (nc - 1) + ROW_HOP * ROW_DEPTH + 1
    per = len(work)

    def row_step(s, carry):
        pl.when((s >= OWN_AT) & (s < OWN_AT + nr))(lambda: ready_own(s - OWN_AT))
        for k in range(2):
            for t in range(NT):
                w = s - ROW_HOP * rdepth[k][t]
                for v in range(nc):
                    @pl.when(w == ROW_STEP * v)
                    def _():
                        @pl.when(rdepth[k][t] == 0)
                        def _():
                            if t == 0:
                                arrive(rowbuf.at[k, 0, v], src_recv.at[k, v])

                        @pl.when(rdepth[k][t] > 0)
                        def _():
                            for h in range(2):
                                ref = rowbuf.at[k, h, v, pl.ds(t * qr, qr)]
                                arrive(ref, row_recv.at[k, h, t, v])

                        send_row(k, t, v)
                        if v == nc - 1:
                            @pl.when(rdepth[k][t] > 0)
                            def _():
                                give_copy(k, t).start()

        for i in range(row_last - work_at):
            part = work[i * per:(i + 1) * per]
            if part:
                @pl.when(col_root & (s == work_at + i))
                def _():
                    for item in part:
                        item()
        return carry

    @pl.when(column_core)
    def _():
        lax.fori_loop(0, chunks + xs_rounds + HOP * COL_DEPTH, col_step, 0)
        for k in range(2):
            @pl.when(jnp.logical_not(row_root[k]))
            def _():
                for t in range(NT):
                    ref = rowbuf.at[k, 0, pl.ds(0, nc), pl.ds(t * qr, qr)]
                    arrive(ref, give_recv.at[k, t])

    @pl.when(row_core)
    def _():
        lax.fori_loop(0, row_last, row_step, 0)

        def have(u, carry):
            arrive(colbuf.at[0, u], sib_recv.at[0, u])
            pl.when(jnp.logical_not(col_root))(functools.partial(arrive, colbuf.at[1, u], sib_recv.at[1, u]))
            for j in range(2):
                mark(j, u)
            return carry

        lax.fori_loop(0, nr, have, 0)

        @pl.when(jnp.logical_not(col_root))
        def _():
            for m in range(xs_count):
                arrive(xs_chunk(m), xsib_recv.at[m])

    def put_v(k, c, value):
        high, low = split(value)
        vh_out[c, pl.ds(k * width, width)] = high
        vl_out[c, pl.ds(k * width, width)] = low

    def solve(c):
        upper = rowbuf[0, core, c]
        vtmp[1, c] = rowbuf[1, core, c] - mm(xs[2], upper)

        @pl.when(p == 1)
        def _():
            fix_out[c] = vtmp[1, c]

            if c == 0:
                @pl.when(q == 0)
                def _():
                    fix_out[0] = xs[2]

        if c == 0:
            @pl.when(q < 2)
            def _():
                vtmp[1, 0] = jnp.where(q == 1, -1.0, 0.0).astype(jnp.float32) * eye

            upper = jnp.where(q < 2, jnp.where(q == 0, -1.0, 0.0).astype(jnp.float32) * eye, upper)
        vtmp[0, c] = upper

    for c in range(nc):
        solve(c)
    for c in range(nc):
        value = mm(xs[1], vtmp[1, c])
        vtmp[1, c] = value
        put_v(1, c, value)
    for c in range(nc):
        vtmp[0, c] = vtmp[0, c] - mm(xs[3], vtmp[1, c])
    for c in range(nc):
        put_v(0, c, mm(xs[0], vtmp[0, c]))

    @pl.when(column_core)
    def _():
        for j in range(2):
            for t in range(NC_TREES):
                for slot, (has, _) in enumerate(ckids[t]):
                    ref = colbuf.at[0, pl.ds(0, nr // NC_TREES)]
                    pl.when(has & (cnode > 0))(functools.partial(arrive, ref, col_send.at[j, t, slot]))

                @pl.when(col_root)
                def _():
                    for n in range(chunks - PACE, chunks):
                        root_send(j, t, n).wait_send()

            sent = jnp.logical_not(col_root) if j == 1 else (p >= 0)
            pl.when(sent)(functools.partial(arrive, colbuf.at[0], sib_send.at[j]))
        for t in range(NC_TREES):
            sent = len(range(t, xs_count, NC_TREES))
            for slot, (has, _) in enumerate(ckids[t]):
                ref = colbuf.at[0, pl.ds(0, sent), pl.ds(0, qr)]
                pl.when(has)(functools.partial(arrive, ref, xs_send.at[t, slot]))
        given = jnp.logical_not(col_root)
        pl.when(given)(functools.partial(arrive, xs.at[pl.ds(0, XS)], xsib_send))
        for k in range(2):
            pl.when(row_root[k])(functools.partial(arrive, rowbuf.at[0, 0], src_send.at[k]))

    @pl.when(row_core)
    def _():
        for k in range(2):
            for t in range(NT):
                for h in range(2):
                    for slot, (has, _) in enumerate(rkids[k][t]):
                        ref = rowbuf.at[0, 0, pl.ds(0, nc), pl.ds(0, qr)]
                        pl.when(has)(functools.partial(arrive, ref, row_send.at[k, h, t, slot]))
            given = jnp.logical_not(row_root[k])
            pl.when(given)(functools.partial(arrive, rowbuf.at[0, 0], give_send.at[k]))
        pl.when(col_root)(functools.partial(arrive, colbuf.at[0], sib_send.at[1]))

        @pl.when(col_root)
        def _():
            for i in range(XS):
                x_copy(i).wait_send()


def update_kernel(dims, flags, own, cols, vh, vl, fix, out, stage, sem):
    nr, nc, width, shift = dims
    p = lax.axis_index("prow")

    def out_copy(r, source):
        return pltpu.make_async_copy(source, out.at[r], sem.at[r % SLOTS])

    def step(r, carry):
        slot = r % SLOTS
        row = r * 8 + p

        @pl.when(r >= SLOTS)
        def _():
            out_copy(r - SLOTS, stage.at[slot]).wait()

        def subtract(left, rows):
            high, low = split(left)
            for c in range(nc):
                prod = dot(high, vh[c, rows]) + (dot(high, vl[c, rows]) + dot(low, vh[c, rows]))
                stage[slot, c] = own[r, c] - prod
            out_copy(r, stage.at[slot]).start()

        first = flags[r] > 0
        second = flags[nr + r] > 0
        trail = row > 1
        both = trail & first & second
        only_first = trail & first & jnp.logical_not(second)
        only_second = trail & jnp.logical_not(first) & second
        kept = (row == 0) | (trail & jnp.logical_not(first) & jnp.logical_not(second))

        @pl.when(both)
        def _():
            subtract(jnp.concatenate([cols[0, r], cols[1, r]], axis=1), slice(0, 2 * width))

        @pl.when(only_first)
        def _():
            subtract(cols[0, r], slice(0, width))

        @pl.when(only_second)
        def _():
            subtract(cols[1, r], slice(width, 2 * width))

        pl.when(kept)(lambda: out_copy(r, own.at[r]).start())
        pl.when(row == 1)(lambda: out_copy(r, fix).start())
        return carry

    lax.fori_loop(0, nr, step, 0)
    for r in range(nr - SLOTS, nr):
        out_copy(r, stage.at[r % SLOTS]).wait()


def body(values, pattern):
    nr, _, nc, _, width, _ = values.shape
    shift = SHIFT_COEF * math.sqrt(width)
    dims = (nr, nc, width, shift)
    vals = values.reshape(nr, nc, width, width)
    pat = pattern.reshape(nr * nc)
    f32, bf16 = jnp.float32, jnp.bfloat16
    vmem = pl.BlockSpec(memory_space=pltpu.VMEM)
    dma = pltpu.SemaphoreType.DMA
    smem = pl.BlockSpec(memory_space=pltpu.SMEM)
    anywhere = pl.BlockSpec(memory_space=pl.ANY)
    *held, flags = pl.pallas_call(
        functools.partial(comm_kernel, dims),
        out_shape=(
            pltpu.VMEM((2, nr, width, width), f32),
            pltpu.VMEM((nr, nc, width, width), f32),
            pltpu.VMEM((nc, 2 * width, width), bf16),
            pltpu.VMEM((nc, 2 * width, width), bf16),
            pltpu.VMEM((nc, width, width), f32),
            jax.ShapeDtypeStruct((2 * nr,), f32),
        ),
        in_specs=[smem, anywhere],
        out_specs=(vmem, vmem, vmem, vmem, vmem, smem),
        scratch_shapes=[
            pltpu.VMEM((2, 2, nc, width, width), f32),
            pltpu.VMEM((2, nc, width, width), f32),
            pltpu.VMEM((6, width, width), f32),
            dma((nr,)),
            dma((nr + nc,)),
            dma((2, NC_TREES, nr * NT // NC_TREES)),
            dma((2, NC_TREES, 2)),
            dma((2, NC_TREES, nr * NT // NC_TREES)),
            dma((2,)),
            dma((2, nr)),
            dma((2, 2, NT, 2)),
            dma((2, 2, NT, nc)),
            dma((2,)),
            dma((2, nc)),
            dma((2,)),
            dma((2, NT)),
            dma((XS,)),
            dma((XS,)),
            dma((NC_TREES, 2)),
            dma((XS * NT,)),
            dma,
            dma((XS * NT,)),
        ],
        compiler_params=pltpu.CompilerParams(
            collective_id=0, has_side_effects=True, vmem_limit_bytes=40 << 20
        ),
        name="gather_panels",
    )(pat, vals)
    cols, own, vh, vl, fix = [pltpu.with_memory_space_constraint(x, pltpu.VMEM) for x in held]
    out = pl.pallas_call(
        functools.partial(update_kernel, dims),
        out_shape=jax.ShapeDtypeStruct((nr, nc, width, width), f32),
        in_specs=[smem, vmem, vmem, vmem, vmem, vmem],
        out_specs=anywhere,
        scratch_shapes=[pltpu.VMEM((SLOTS, nc, width, width), f32), dma((SLOTS,))],
        compiler_params=pltpu.CompilerParams(vmem_limit_bytes=40 << 20),
        name="update_blocks",
    )(flags, own, cols, vh, vl, fix)
    return out.reshape(values.shape)


def solution(mesh):
    return jax.shard_map(
        body,
        mesh=mesh,
        in_specs=(P(None, "prow", None, "pcol", None, None), P(None, "prow", None, "pcol")),
        out_specs=P(None, "prow", None, "pcol", None, None),
        check_vma=False,
    )
```

```python
import functools
import math

import jax
import jax.numpy as jnp
from jax import lax
from jax.experimental import pallas as pl
from jax.experimental.pallas import tpu as pltpu
from jax.sharding import PartitionSpec as P

SWEEPS = 3
SHIFT_COEF = 5.0
MESH = pl.DeviceIdType.MESH

COL_TREES = (
    ((0, 0, 1, 0), (1, 0, 2, 0), (1, 0, 1, 1), (2, 0, 3, 0), (2, 0, 2, 1), (1, 1, 0, 1), (2, 1, 3, 1)),
    ((0, 0, 3, 0), (3, 0, 2, 0), (3, 0, 3, 1), (2, 0, 1, 0), (3, 1, 2, 1), (3, 1, 0, 1), (2, 1, 1, 1)),
    ((0, 0, 0, 1), (0, 1, 1, 1), (0, 1, 3, 1), (1, 1, 2, 1), (1, 1, 1, 0), (3, 1, 3, 0), (2, 1, 2, 0)),
)
NC_TREES = len(COL_TREES)
TREES = (
    ((0, 0, 1, 0), (1, 0, 2, 0), (1, 0, 1, 1), (2, 0, 3, 0), (1, 1, 2, 1), (1, 1, 0, 1), (2, 1, 3, 1)),
    ((0, 0, 3, 0), (3, 0, 2, 0), (3, 0, 3, 1), (2, 0, 1, 0), (3, 1, 2, 1), (3, 1, 0, 1), (2, 1, 1, 1)),
    ((0, 0, 1, 0), (1, 0, 2, 0), (2, 0, 3, 0), (2, 0, 2, 1), (2, 1, 3, 1), (2, 1, 1, 1), (3, 1, 0, 1)),
    ((0, 0, 3, 0), (0, 0, 0, 1), (3, 0, 2, 0), (0, 1, 1, 1), (0, 1, 3, 1), (2, 0, 1, 0), (1, 1, 2, 1)),
)
NT = len(TREES)
HOP = 4
ROW_HOP = 2
ROW_STEP = 3
PACE = 4
XS = 4
OWN_AT = 3
SLOTS = 6


def tree_depths(edges):
    depth = {(0, 0): 0}
    for a, b, c, d in edges:
        depth[c, d] = depth[a, b] + 1
    return depth


COL_DEPTHS = tuple(tree_depths(edges) for edges in COL_TREES)
DEPTHS = tuple(tree_depths(edges) for edges in TREES)
COL_DEPTH = max(max(d.values()) for d in COL_DEPTHS)
ROW_DEPTH = max(max(d.values()) for d in DEPTHS)


def lookup(node, table):
    out = jnp.int32(0)
    for (a, b), value in table.items():
        if value:
            out = jnp.where(node == a * 2 + b, jnp.int32(value), out)
    return out


def split(x):
    high = x.astype(jnp.bfloat16)
    return high, (x - high.astype(jnp.float32)).astype(jnp.bfloat16)


def dot(a, b):
    return jnp.dot(a, b, preferred_element_type=jnp.float32)


def mm(a, b):
    ah, al = split(a)
    bh, bl = split(b)
    return dot(ah, bh) + (dot(ah, bl) + dot(al, bh))


def eye_of(width):
    rows = lax.broadcasted_iota(jnp.int32, (width, width), 0)
    cols = lax.broadcasted_iota(jnp.int32, (width, width), 1)
    return jnp.where(rows == cols, 1.0, 0.0).astype(jnp.float32)


def comm_kernel(
    dims, pat, values, colbuf, own, vh_out, vl_out, fix_out, flags,
    rowbuf, vtmp, xs,
    own_sem, load_sem, root_sem, col_send, col_recv, sib_send, sib_recv,
    row_send, row_recv, src_send, src_recv, give_send, give_recv,
    x_send, x_recv, xs_send, xs_recv, xsib_send, xsib_recv,
):
    nr, nc, width, shift = dims
    qr = width // NT
    chunks = nr * NT // NC_TREES
    p = lax.axis_index("prow")
    q = lax.axis_index("pcol")
    xlo, z = p // 4, p % 4
    y, xhi, core = q // 4, (q // 2) % 2, q % 2

    def dev(xlo_, z_, y_, xhi_, core_):
        return (xlo_ * 4 + z_, y_ * 4 + xhi_ * 2 + core_)

    sibling = dev(xlo, z, y, xhi, 1 - core)
    barrier = pltpu.get_barrier_semaphore()
    partners = (
        sibling,
        dev(xlo, z, (y + 1) % 4, xhi, core),
        dev(xlo, z, (y + 3) % 4, xhi, core),
        dev(xlo, z, y, 1 - xhi, core),
        dev(xlo, (z + 1) % 4, y, xhi, core),
        dev(xlo, (z + 3) % 4, y, xhi, core),
        dev(1 - xlo, z, y, xhi, core),
    )
    for partner in partners:
        pl.semaphore_signal(barrier, inc=1, device_id=partner, device_id_type=MESH)

    cnode = y * 2 + xhi
    cdepth = [lookup(cnode, d) for d in COL_DEPTHS]
    rnode = [((z + 4 - k) % 4) * 2 + xlo for k in range(2)]
    rdepth = [[lookup(rnode[k], d) for d in DEPTHS] for k in range(2)]

    def children(edges, node, place):
        kids = {}
        for a, b, c, d in edges:
            kids.setdefault((a, b), []).append((c, d))
        out = []
        for slot in range(max(len(v) for v in kids.values())):
            has = {n: 1 for n, v in kids.items() if len(v) > slot}
            to_a = lookup(node, {n: v[slot][0] for n, v in kids.items() if len(v) > slot})
            to_b = lookup(node, {n: v[slot][1] for n, v in kids.items() if len(v) > slot})
            out.append((lookup(node, has) == 1, place(to_a, to_b)))
        return out

    ckids = [children(e, cnode, lambda a, b: dev(xlo, z, a, b, core)) for e in COL_TREES]
    rkids = [
        [children(e, rnode[k], lambda a, b, k=k: dev(b, (a + k) % 4, y, xhi, core)) for e in TREES]
        for k in range(2)
    ]

    def remote(src, dst, send, recv, device):
        return pltpu.make_async_remote_copy(
            src_ref=src, dst_ref=dst, send_sem=send, recv_sem=recv,
            device_id=device, device_id_type=MESH,
        )

    def arrive(ref, sem):
        pltpu.make_async_copy(ref, ref, sem).wait()

    eye = eye_of(width)
    col_root = cnode == 0
    row_root = [p == k for k in range(2)]
    column_core, row_core = core == 0, core == 1

    def block_of(n, t):
        return NC_TREES * (n // NT) + t

    def col_chunk(j, t, n):
        return colbuf.at[j, block_of(n, t), pl.ds((n % NT) * qr, qr)]

    def send_col(j, t, n):
        ref = col_chunk(j, t, n)
        for slot, (has, device) in enumerate(ckids[t]):
            pl.when(has)(remote(ref, ref, col_send.at[j, t, slot], col_recv.at[j, t, n], device).start)

    def root_send(j, t, n):
        ref = col_chunk(j, t, n)
        return remote(ref, ref, root_sem.at[j, t, n], col_recv.at[j, t, n], ckids[t][0][1])

    def sib_copy(j, u):
        ref = colbuf.at[j, u]
        return remote(ref, ref, sib_send.at[j], sib_recv.at[j, u], sibling)

    def send_row(k, t, v):
        for h in range(2):
            ref = rowbuf.at[k, h, v, pl.ds(t * qr, qr)]
            for slot, (has, device) in enumerate(rkids[k][t]):
                sems = row_send.at[k, h, t, slot], row_recv.at[k, h, t, v]
                pl.when(has)(remote(ref, ref, *sems, device).start)

    def xs_chunk(m):
        return xs.at[m // NT, pl.ds((m % NT) * qr, qr)]

    def send_xs(t, m):
        ref = xs_chunk(m)
        for slot, (has, device) in enumerate(ckids[t]):
            pl.when(has)(remote(ref, ref, xs_send.at[t, slot], xs_recv.at[m], device).start)

    def src_copy(k, v):
        ref = rowbuf.at[k, 0, v]
        return remote(ref, ref, src_send.at[k], src_recv.at[k, v], sibling)

    def give_copy(k, t):
        ref = rowbuf.at[k, 0, pl.ds(0, nc), pl.ds(t * qr, qr)]
        return remote(ref, ref, give_send.at[k], give_recv.at[k, t], sibling)

    def x_copy(i):
        ref = xs.at[i]
        return remote(ref, ref, x_send.at[i], x_recv.at[i], sibling)

    def load_col(u):
        return pltpu.make_async_copy(values.at[u, 0], colbuf.at[core, u], load_sem.at[u])

    def load_row(k, v):
        return pltpu.make_async_copy(values.at[0, v], rowbuf.at[k, core, v], load_sem.at[nr + v])

    def load_own(u):
        return pltpu.make_async_copy(values.at[u], own.at[u], own_sem.at[u])

    def ready_col(u):
        load_col(u).wait()
        on_diag = (u == 0) & (p == core)
        block = colbuf[core, u] * pat[u * nc].astype(jnp.float32)
        colbuf[core, u] = block + jnp.where(on_diag, shift, 0.0).astype(jnp.float32) * eye

    def ready_own(u):
        load_own(u).wait()
        row = u * 8 + p
        for c in range(nc):
            keep = pat[u * nc + c].astype(jnp.float32)
            if c == 0:
                keep = jnp.where((q < 2) & (row > 1), 0.0, keep)
            own[u, c] = own[u, c] * keep

            @pl.when(row == c * 16 + q)
            def _():
                own[u, c] += shift * eye

    @pl.when(col_root)
    def _():
        for u in range(nr):
            load_col(u).start()

    for k in range(2):
        @pl.when(row_root[k])
        def _():
            for v in range(nc):
                load_row(k, v).start()

    for u in range(nr):
        load_own(u).start()

    pl.semaphore_wait(barrier, len(partners))

    @pl.when(col_root & row_core)
    def _():
        def one(u, carry):
            ready_col(u)
            sib_copy(1, u).start()
            return carry

        lax.fori_loop(0, nr, one, 0)

    for k in range(2):
        @pl.when(row_root[k])
        def _():
            for v in range(nc):
                load_row(k, v).wait()
                block = rowbuf[k, core, v] * pat[v].astype(jnp.float32)
                if v == 0:
                    block = block + jnp.where(q == k, shift, 0.0).astype(jnp.float32) * eye
                rowbuf[k, core, v] = block

                @pl.when(column_core)
                def _():
                    src_copy(k, v).start()

    def mark(j, u):
        flags[j * nr + u] = jnp.max(jnp.abs(colbuf[j, u]))

    xs_count = XS * NT
    xs_rounds = -(-xs_count // NC_TREES)

    def col_step(s, carry):
        pl.when((s >= OWN_AT) & (s < OWN_AT + nr))(lambda: ready_own(s - OWN_AT))
        for t in range(NC_TREES):
            n = s - HOP * cdepth[t]
            m = (n - chunks) * NC_TREES + t

            @pl.when((n >= chunks) & (m < xs_count))
            def _():
                @pl.when(cdepth[t] > 0)
                def _():
                    arrive(xs_chunk(m), xs_recv.at[m])

                if t == 0:
                    @pl.when((cdepth[t] == 0) & (n == chunks))
                    def _():
                        for i in range(XS):
                            arrive(xs.at[i], x_recv.at[i])

                send_xs(t, m)

                @pl.when(cdepth[t] > 0)
                def _():
                    ref = xs_chunk(m)
                    remote(ref, ref, xsib_send, xsib_recv.at[m], sibling).start()

            @pl.when((n >= 0) & (n < chunks))
            def _():
                u = block_of(n, t)
                for j in range(2):
                    @pl.when(cdepth[t] > 0)
                    def _():
                        arrive(col_chunk(j, t, n), col_recv.at[j, t, n])
                        send_col(j, t, n)

                        @pl.when(n % NT == NT - 1)
                        def _():
                            sib_copy(j, u).start()
                            mark(j, u)

                    @pl.when(cdepth[t] == 0)
                    def _():
                        @pl.when(n % NT == 0)
                        def _():
                            if j == 0:
                                ready_col(u)
                                sib_copy(0, u).start()
                            else:
                                arrive(colbuf.at[1, u], sib_recv.at[1, u])
                            mark(j, u)

                        @pl.when(n >= PACE)
                        def _():
                            root_send(j, t, n - PACE).wait_send()

                        root_send(j, t, n).start()

        return carry

    def newton_steps(block_ref, out):
        def first():
            block = block_ref[...]
            xs[out] = (2.0 * eye - block * (1.0 / shift)) * (1.0 / shift)

        def inner():
            xs[5] = 2.0 * eye - mm(block_ref[...], xs[out])

        def outer():
            xs[out] = mm(xs[out], xs[5])

        steps = [first]
        for _ in range(SWEEPS - 1):
            steps += [inner, outer]
        return steps

    def middle():
        xs[2] = mm(rowbuf[1, 0, 0], xs[0])

    def schur():
        xs[4] = rowbuf[1, 1, 0] - mm(xs[2], rowbuf[0, 1, 0])

    def corner():
        xs[3] = rowbuf[0, 1, 0]
        x_copy(3).start()

    work = [corner]
    work += newton_steps(rowbuf.at[0, 0, 0], 0)
    work += [x_copy(0).start, middle, x_copy(2).start, schur]
    work += newton_steps(xs.at[4], 1)
    work += [x_copy(1).start]

    deepest = rdepth[0][0]
    for d in rdepth[0] + rdepth[1]:
        deepest = jnp.maximum(deepest, d)
    row_last = ROW_STEP * (nc - 1) + ROW_HOP * ROW_DEPTH + 1

    def row_step(s, carry):
        pl.when((s >= OWN_AT) & (s < OWN_AT + nr))(lambda: ready_own(s - OWN_AT))
        for k in range(2):
            for t in range(NT):
                w = s - ROW_HOP * rdepth[k][t]
                for v in range(nc):
                    @pl.when(w == ROW_STEP * v)
                    def _():
                        @pl.when(rdepth[k][t] == 0)
                        def _():
                            if t == 0:
                                arrive(rowbuf.at[k, 0, v], src_recv.at[k, v])

                        @pl.when(rdepth[k][t] > 0)
                        def _():
                            for h in range(2):
                                ref = rowbuf.at[k, h, v, pl.ds(t * qr, qr)]
                                arrive(ref, row_recv.at[k, h, t, v])

                        send_row(k, t, v)
                        if v == nc - 1:
                            @pl.when(rdepth[k][t] > 0)
                            def _():
                                give_copy(k, t).start()

        @pl.when(col_root & (s == ROW_HOP * deepest))
        def _():
            for item in work:
                item()

        return carry

    @pl.when(column_core)
    def _():
        lax.fori_loop(0, chunks + xs_rounds + HOP * COL_DEPTH, col_step, 0)
        for k in range(2):
            @pl.when(jnp.logical_not(row_root[k]))
            def _():
                for t in range(NT):
                    ref = rowbuf.at[k, 0, pl.ds(0, nc), pl.ds(t * qr, qr)]
                    arrive(ref, give_recv.at[k, t])

    @pl.when(row_core)
    def _():
        lax.fori_loop(0, row_last, row_step, 0)

        def have(u, carry):
            arrive(colbuf.at[0, u], sib_recv.at[0, u])
            pl.when(jnp.logical_not(col_root))(functools.partial(arrive, colbuf.at[1, u], sib_recv.at[1, u]))
            for j in range(2):
                mark(j, u)
            return carry

        lax.fori_loop(0, nr, have, 0)

        @pl.when(jnp.logical_not(col_root))
        def _():
            for m in range(xs_count):
                arrive(xs_chunk(m), xsib_recv.at[m])

    def put_v(k, c, value):
        high, low = split(value)
        vh_out[c, pl.ds(k * width, width)] = high
        vl_out[c, pl.ds(k * width, width)] = low

    def solve(c):
        upper = rowbuf[0, core, c]
        vtmp[1, c] = rowbuf[1, core, c] - mm(xs[2], upper)

        @pl.when(p == 1)
        def _():
            fix_out[c] = vtmp[1, c]

            if c == 0:
                @pl.when(q == 0)
                def _():
                    fix_out[0] = xs[2]

        if c == 0:
            @pl.when(q < 2)
            def _():
                vtmp[1, 0] = jnp.where(q == 1, -1.0, 0.0).astype(jnp.float32) * eye

            upper = jnp.where(q < 2, jnp.where(q == 0, -1.0, 0.0).astype(jnp.float32) * eye, upper)
        vtmp[0, c] = upper

    for c in range(nc):
        solve(c)
    for c in range(nc):
        value = mm(xs[1], vtmp[1, c])
        vtmp[1, c] = value
        put_v(1, c, value)
    for c in range(nc):
        vtmp[0, c] = vtmp[0, c] - mm(xs[3], vtmp[1, c])
    for c in range(nc):
        put_v(0, c, mm(xs[0], vtmp[0, c]))

    @pl.when(column_core)
    def _():
        for j in range(2):
            for t in range(NC_TREES):
                for slot, (has, _) in enumerate(ckids[t]):
                    ref = colbuf.at[0, pl.ds(0, nr // NC_TREES)]
                    pl.when(has & (cnode > 0))(functools.partial(arrive, ref, col_send.at[j, t, slot]))

                @pl.when(col_root)
                def _():
                    for n in range(chunks - PACE, chunks):
                        root_send(j, t, n).wait_send()

            sent = jnp.logical_not(col_root) if j == 1 else (p >= 0)
            pl.when(sent)(functools.partial(arrive, colbuf.at[0], sib_send.at[j]))
        for t in range(NC_TREES):
            sent = len(range(t, xs_count, NC_TREES))
            for slot, (has, _) in enumerate(ckids[t]):
                ref = colbuf.at[0, pl.ds(0, sent), pl.ds(0, qr)]
                pl.when(has)(functools.partial(arrive, ref, xs_send.at[t, slot]))
        given = jnp.logical_not(col_root)
        pl.when(given)(functools.partial(arrive, xs.at[pl.ds(0, XS)], xsib_send))
        for k in range(2):
            pl.when(row_root[k])(functools.partial(arrive, rowbuf.at[0, 0], src_send.at[k]))

    @pl.when(row_core)
    def _():
        for k in range(2):
            for t in range(NT):
                for h in range(2):
                    for slot, (has, _) in enumerate(rkids[k][t]):
                        ref = rowbuf.at[0, 0, pl.ds(0, nc), pl.ds(0, qr)]
                        pl.when(has)(functools.partial(arrive, ref, row_send.at[k, h, t, slot]))
            given = jnp.logical_not(row_root[k])
            pl.when(given)(functools.partial(arrive, rowbuf.at[0, 0], give_send.at[k]))
        pl.when(col_root)(functools.partial(arrive, colbuf.at[0], sib_send.at[1]))

        @pl.when(col_root)
        def _():
            for i in range(XS):
                x_copy(i).wait_send()


def update_kernel(dims, flags, own, cols, vh, vl, fix, out, stage, sem):
    nr, nc, width, shift = dims
    p = lax.axis_index("prow")

    def out_copy(r, source):
        return pltpu.make_async_copy(source, out.at[r], sem.at[r % SLOTS])

    def step(r, carry):
        slot = r % SLOTS
        row = r * 8 + p

        @pl.when(r >= SLOTS)
        def _():
            out_copy(r - SLOTS, stage.at[slot]).wait()

        def subtract(left, rows):
            high, low = split(left)
            for c in range(nc):
                prod = dot(high, vh[c, rows]) + (dot(high, vl[c, rows]) + dot(low, vh[c, rows]))
                stage[slot, c] = own[r, c] - prod
            out_copy(r, stage.at[slot]).start()

        first = flags[r] > 0
        second = flags[nr + r] > 0
        trail = row > 1
        both = trail & first & second
        only_first = trail & first & jnp.logical_not(second)
        only_second = trail & jnp.logical_not(first) & second
        kept = (row == 0) | (trail & jnp.logical_not(first) & jnp.logical_not(second))

        @pl.when(both)
        def _():
            subtract(jnp.concatenate([cols[0, r], cols[1, r]], axis=1), slice(0, 2 * width))

        @pl.when(only_first)
        def _():
            subtract(cols[0, r], slice(0, width))

        @pl.when(only_second)
        def _():
            subtract(cols[1, r], slice(width, 2 * width))

        pl.when(kept)(lambda: out_copy(r, own.at[r]).start())
        pl.when(row == 1)(lambda: out_copy(r, fix).start())
        return carry

    lax.fori_loop(0, nr, step, 0)
    for r in range(nr - SLOTS, nr):
        out_copy(r, stage.at[r % SLOTS]).wait()


def body(values, pattern):
    nr, _, nc, _, width, _ = values.shape
    shift = SHIFT_COEF * math.sqrt(width)
    dims = (nr, nc, width, shift)
    vals = values.reshape(nr, nc, width, width)
    pat = pattern.reshape(nr * nc)
    f32, bf16 = jnp.float32, jnp.bfloat16
    vmem = pl.BlockSpec(memory_space=pltpu.VMEM)
    dma = pltpu.SemaphoreType.DMA
    smem = pl.BlockSpec(memory_space=pltpu.SMEM)
    anywhere = pl.BlockSpec(memory_space=pl.ANY)
    *held, flags = pl.pallas_call(
        functools.partial(comm_kernel, dims),
        out_shape=(
            pltpu.VMEM((2, nr, width, width), f32),
            pltpu.VMEM((nr, nc, width, width), f32),
            pltpu.VMEM((nc, 2 * width, width), bf16),
            pltpu.VMEM((nc, 2 * width, width), bf16),
            pltpu.VMEM((nc, width, width), f32),
            jax.ShapeDtypeStruct((2 * nr,), f32),
        ),
        in_specs=[smem, anywhere],
        out_specs=(vmem, vmem, vmem, vmem, vmem, smem),
        scratch_shapes=[
            pltpu.VMEM((2, 2, nc, width, width), f32),
            pltpu.VMEM((2, nc, width, width), f32),
            pltpu.VMEM((6, width, width), f32),
            dma((nr,)),
            dma((nr + nc,)),
            dma((2, NC_TREES, nr * NT // NC_TREES)),
            dma((2, NC_TREES, 2)),
            dma((2, NC_TREES, nr * NT // NC_TREES)),
            dma((2,)),
            dma((2, nr)),
            dma((2, 2, NT, 2)),
            dma((2, 2, NT, nc)),
            dma((2,)),
            dma((2, nc)),
            dma((2,)),
            dma((2, NT)),
            dma((XS,)),
            dma((XS,)),
            dma((NC_TREES, 2)),
            dma((XS * NT,)),
            dma,
            dma((XS * NT,)),
        ],
        compiler_params=pltpu.CompilerParams(
            collective_id=0, has_side_effects=True, vmem_limit_bytes=40 << 20
        ),
        name="gather_panels",
    )(pat, vals)
    cols, own, vh, vl, fix = [pltpu.with_memory_space_constraint(x, pltpu.VMEM) for x in held]
    out = pl.pallas_call(
        functools.partial(update_kernel, dims),
        out_shape=jax.ShapeDtypeStruct((nr, nc, width, width), f32),
        in_specs=[smem, vmem, vmem, vmem, vmem, vmem],
        out_specs=anywhere,
        scratch_shapes=[pltpu.VMEM((SLOTS, nc, width, width), f32), dma((SLOTS,))],
        compiler_params=pltpu.CompilerParams(vmem_limit_bytes=40 << 20),
        name="update_blocks",
    )(flags, own, cols, vh, vl, fix)
    return out.reshape(values.shape)


def solution(mesh):
    return jax.shard_map(
        body,
        mesh=mesh,
        in_specs=(P(None, "prow", None, "pcol", None, None), P(None, "prow", None, "pcol")),
        out_specs=P(None, "prow", None, "pcol", None, None),
        check_vma=False,
    )
```
